512 devices in a mesh: depth: 64 (over z_hi, y, core), height: 8 (over z_lo, x).
Axes of the slice: x: 4, y: 8, z: 8 (z_hi: 4, z_lo: 2; z = z_hi * 2 + z_lo), core: 2. Of those that a mesh axis runs over, the one named last changes fastest.
Arguments:
- features: bfloat16 [32, 256, 32, 128], P(None, 'depth', 'height'), may hold values from -6 to 6
- kernel_in: bfloat16 [27648], replicated, may hold values from -0.21875 to 0.21875
- kernel_down: bfloat16 [55296], replicated, may hold values from -0.21875 to 0.21875
- kernel_coarse: bfloat16 [110592], replicated, may hold values from -0.15625 to 0.15625
- kernel_up: bfloat16 [110592], replicated, may hold values from -0.15625 to 0.15625
- kernel_out: bfloat16 [27648], replicated, may hold values from -0.21875 to 0.21875
- projection: bfloat16 [64, 32], replicated, may hold values from -0.75 to 0.75
- biases: float32 [256], replicated, may hold values from -3 to 3
- cotangent: bfloat16 [32, 256, 32, 128], P(None, 'depth', 'height'), may hold values from -6 to 6
Outputs:
- decoded: bfloat16 [32, 256, 32, 128], P(None, 'depth', 'height')
- grad_features: bfloat16 [32, 256, 32, 128], P(None, 'depth', 'height')
- grad_in: float32 [27648], replicated
- grad_down: float32 [55296], replicated
- grad_coarse: float32 [110592], replicated
- grad_up: float32 [110592], replicated
- grad_out: float32 [27648], replicated
- grad_projection: float32 [64, 32], replicated
- grad_biases: float32 [256], replicated
The draws below stay inside these ranges and needn't reach their ends.
All inputs are finite; a program needn't handle non-finite values.
Results may differ from the reference program's by a relative error of at most 0.025.
Values may be sent and summed in bfloat16 or wider, within the bound.
No kernel may reach another device: no remote copies, remote signals or barrier semaphores. Data moves between devices by JAX's collectives and lax.ppermute only.
A program may use at most 64 MiB of HBM per device.

```python
import jax
import jax.numpy as jnp
from jax import lax

CH_FINE = 32
CH_MID = 64
WIDTH_ALL = 128
DEPTH_ALL = 256
HEIGHT_ALL = 32
BIAS_ALL = 256


def block_scale(key, extent, shards, low, largest):
    def one(axis_at, blocks):
        steps = jax.random.uniform(jax.random.fold_in(jax.random.fold_in(key, 6), axis_at), (blocks,), jnp.float32, low / len(shards), largest / len(shards))
        return jnp.repeat(jnp.exp(steps), extent[axis_at] // blocks).reshape((-1,) + (1,) * (len(extent) - axis_at - 1))

    gain = one(*shards[0])
    for cut in shards[1:]:
        gain = gain * one(*cut)
    return gain


def noise(rng, shape, spread, limit, shards=(), held_as=jnp.bfloat16):
    loudness = block_scale(rng, shape, shards, -0.22, 0.18) if shards else 1.0
    entries = jax.random.normal(rng, shape, jnp.float32) * spread * loudness
    return jnp.minimum(jnp.maximum(entries, -limit), limit).astype(held_as)


def setup_inputs(seed: int = 0) -> dict:
    arg_keys = jax.random.split(jax.random.key(seed), 10)
    return {
        "features": noise(arg_keys[0], (CH_FINE, DEPTH_ALL, HEIGHT_ALL, WIDTH_ALL), 1.0, 6.0, ((1, 64), (2, 8))),
        "kernel_in": noise(arg_keys[1], (27 * CH_FINE * CH_FINE,), (27 * CH_FINE) ** -0.5, 0.21875),
        "kernel_down": noise(arg_keys[2], (27 * CH_MID * CH_FINE,), (27 * CH_FINE) ** -0.5, 0.21875),
        "kernel_coarse": noise(arg_keys[3], (27 * CH_MID * CH_MID,), (27 * CH_MID) ** -0.5, 0.15625),
        "kernel_up": noise(arg_keys[4], (27 * CH_MID * CH_MID,), (27 * CH_MID) ** -0.5, 0.15625),
        "kernel_out": noise(arg_keys[5], (27 * CH_FINE * CH_FINE,), (27 * CH_FINE) ** -0.5, 0.21875),
        "projection": noise(arg_keys[6], (CH_MID, CH_FINE), CH_MID ** -0.5, 0.75),
        "biases": noise(arg_keys[7], (BIAS_ALL,), 0.5, 3.0, (), jnp.float32),
        "cotangent": noise(arg_keys[8], (CH_FINE, DEPTH_ALL, HEIGHT_ALL, WIDTH_ALL), 1.0, 6.0, ((1, 64), (2, 8))),
    }


def shaped(flat, outs, ins):
    return flat.reshape(3, 3, outs, 3 * ins)

def conv_full(volume, kern):
    outs = kern.shape[2]
    ins = kern.shape[3] // 3
    weights = kern.astype(jnp.float32).reshape(3, 3, outs, 3, ins).transpose(2, 4, 0, 1, 3)
    result = lax.conv_general_dilated(volume.astype(jnp.float32)[None], weights, (1, 1, 1), ((1, 1), (1, 1), (1, 1)), dimension_numbers=('NCDHW', 'OIDHW', 'NCDHW'), precision=lax.Precision.HIGHEST)
    return result[0]

def flipped(kern):
    outs = kern.shape[2]
    ins = kern.shape[3] // 3
    turned = kern.reshape(3, 3, outs, 3, ins)[::-1, ::-1, :, ::-1, :]
    return turned.transpose(0, 1, 4, 3, 2).reshape(3, 3, ins, 3 * outs)

def kernel_full(volume, grad, kern):
    source = volume.astype(jnp.float32)
    _, pull = jax.vjp(lambda weights: conv_full(source, weights), kern.astype(jnp.float32))
    return pull(grad.astype(jnp.float32))[0].reshape(-1)

def pool_sum(volume):
    chans, span_d, span_h, span_w = volume.shape
    blocks = volume.astype(jnp.float32).reshape(chans, span_d // 2, 2, span_h // 2, 2, span_w // 2, 2)
    return lax.optimization_barrier(jnp.sum(blocks, axis=(2, 4, 6)))

def upsample(volume):
    return jnp.repeat(jnp.repeat(jnp.repeat(volume, 2, axis=1), 2, axis=2), 2, axis=3)

def silu_grad(value):
    sigma = jax.nn.sigmoid(value)
    return sigma * (1.0 + value * (1.0 - sigma))

def column(vector):
    return vector[:, None, None, None]

def reference(features, kernel_in, kernel_down, kernel_coarse, kernel_up, kernel_out, projection, biases, cotangent):
    fine = CH_FINE
    middle = CH_MID
    kernel_in = shaped(kernel_in, fine, fine)
    kernel_down = shaped(kernel_down, middle, fine)
    kernel_coarse = shaped(kernel_coarse, middle, middle)
    kernel_up = shaped(kernel_up, middle, middle)
    kernel_out = shaped(kernel_out, fine, fine)
    bias_in = biases[:fine]
    bias_down = biases[fine:fine + middle]
    bias_coarse = biases[fine + middle:fine + 2 * middle]
    bias_up = biases[fine + 2 * middle:fine + 3 * middle]
    bias_out = biases[fine + 3 * middle:]
    bf = jnp.bfloat16
    f32 = jnp.float32
    pre_first = conv_full(features, kernel_in) + column(bias_in)
    act_first = jax.nn.silu(pre_first).astype(bf)
    pooled_one = (pool_sum(act_first) * 0.125).astype(bf)
    pre_second = conv_full(pooled_one, kernel_down) + column(bias_down)
    act_second = jax.nn.silu(pre_second).astype(bf)
    pooled_two = (pool_sum(act_second) * 0.125).astype(bf)
    pre_third = conv_full(pooled_two, kernel_coarse) + column(bias_coarse)
    act_third = jax.nn.silu(pre_third).astype(bf)
    merged = (act_second.astype(f32) + upsample(act_third).astype(f32)).astype(bf)
    pre_fourth = conv_full(merged, kernel_up) + column(bias_up)
    act_fourth = jax.nn.silu(pre_fourth).astype(bf)
    lifted = jnp.einsum('io,idhw->odhw', projection.astype(f32), act_fourth.astype(f32), precision=lax.Precision.HIGHEST)
    skip_sum = (act_first.astype(f32) + upsample(lifted)).astype(bf)
    decoded = (conv_full(skip_sum, kernel_out) + column(bias_out)).astype(bf)
    grad_skip = conv_full(cotangent, flipped(kernel_out)).astype(bf)
    grad_lift = pool_sum(grad_skip)
    grad_act4 = jnp.einsum('io,odhw->idhw', projection.astype(f32), grad_lift, precision=lax.Precision.HIGHEST)
    grad_pre4 = (grad_act4 * silu_grad(pre_fourth)).astype(bf)
    grad_merged = conv_full(grad_pre4, flipped(kernel_up))
    grad_pre3 = (pool_sum(grad_merged) * silu_grad(pre_third)).astype(bf)
    grad_pool2 = conv_full(grad_pre3, flipped(kernel_coarse))
    grad_pre2 = ((grad_merged + upsample(grad_pool2) * 0.125) * silu_grad(pre_second)).astype(bf)
    grad_pool1 = conv_full(grad_pre2, flipped(kernel_down))
    grad_pre1 = ((grad_skip.astype(f32) + upsample(grad_pool1) * 0.125) * silu_grad(pre_first)).astype(bf)
    grad_features = conv_full(grad_pre1, flipped(kernel_in)).astype(bf)
    scale = 1.0 / jnp.sqrt(jnp.asarray(features.shape[1] * features.shape[2] * features.shape[3], f32))
    grad_in = kernel_full(features, grad_pre1, kernel_in) * scale
    grad_down = kernel_full(pooled_one, grad_pre2, kernel_down) * scale
    grad_coarse = kernel_full(pooled_two, grad_pre3, kernel_coarse) * scale
    grad_up = kernel_full(merged, grad_pre4, kernel_up) * scale
    grad_out = kernel_full(skip_sum, cotangent, kernel_out) * scale
    grad_projection = jnp.einsum('idhw,odhw->io', act_fourth.astype(f32), grad_lift, precision=lax.Precision.HIGHEST) * scale
    parts = [lax.optimization_barrier(jnp.sum(item.astype(f32), axis=(1, 2, 3))) for item in (grad_pre1, grad_pre2, grad_pre3, grad_pre4, cotangent)]
    grad_biases = jnp.concatenate(parts) * scale
    return (decoded, grad_features, grad_in, grad_down, grad_coarse, grad_up, grad_out, grad_projection, grad_biases)
```

```python
import math

import jax
import jax.numpy as jnp
from jax import lax
from jax.sharding import PartitionSpec as P

CH_FINE = 32
CH_MID = 64


def padded_2(cells, sides, width):
    for axis, dim in sides:
        count = lax.axis_size(axis)
        ends = count - 1
        head = lax.slice_in_dim(cells, 0, width, axis=dim)
        tail = lax.slice_in_dim(cells, cells.shape[dim] - width, cells.shape[dim], axis=dim)
        cells = jnp.concatenate(
            [
                lax.ppermute(tail, axis, [(i, (i + 1) % count) for i in range(ends)]),
                cells,
                lax.ppermute(head, axis, [((i + 1) % count, i) for i in range(ends)]),
            ],
            axis=dim,
        )
    return cells


def extend(volume):
    both_ext = padded_2(volume, (("depth", 1), ("height", 2)), 1)
    return jnp.pad(both_ext, ((0, 0), (0, 0), (0, 0), (1, 1)))


def shaped(flat, outs, ins):
    return flat.reshape(3, 3, outs, 3 * ins)


def widened(padded):
    span_w = padded.shape[3] - 2
    pieces = [padded[:, :, :, tap_width : tap_width + span_w] for tap_width in range(3)]
    return jnp.concatenate(pieces, axis=0)


def conv_taps(padded, kern):
    span_d = padded.shape[1] - 2
    span_h = padded.shape[2] - 2
    wide = widened(padded)
    result = None
    for tap_depth in range(3):
        for tap_height in range(3):
            window = wide[:, tap_depth : tap_depth + span_d, tap_height : tap_height + span_h, :]
            term = jnp.einsum(
                "ok,kdhw->odhw",
                kern[tap_depth, tap_height],
                window,
                preferred_element_type=jnp.float32,
            )
            result = term if result is None else result + term
    return result


def kernel_taps(padded, grad):
    span_d = padded.shape[1] - 2
    span_h = padded.shape[2] - 2
    wide = widened(padded)
    rows = []
    for tap_depth in range(3):
        inner = []
        for tap_height in range(3):
            window = wide[:, tap_depth : tap_depth + span_d, tap_height : tap_height + span_h, :]
            inner.append(
                jnp.einsum("odhw,kdhw->ok", grad, window, preferred_element_type=jnp.float32)
            )
        rows.append(jnp.stack(inner))
    return jnp.stack(rows).reshape(-1)


def flipped(kern):
    outs = kern.shape[2]
    ins = kern.shape[3] // 3
    turned = kern.reshape(3, 3, outs, 3, ins)[::-1, ::-1, :, ::-1, :]
    return turned.transpose(0, 1, 4, 3, 2).reshape(3, 3, ins, 3 * outs)


def pool_sum(volume):
    chans, span_d, span_h, span_w = volume.shape
    blocks = volume.astype(jnp.float32).reshape(
        chans, span_d // 2, 2, span_h // 2, 2, span_w // 2, 2
    )
    return jnp.sum(blocks, axis=(2, 4, 6))


def upsample(volume):
    chans, span_d, span_h, span_w = volume.shape
    spread = jnp.broadcast_to(
        volume[:, :, None, :, None, :, None], (chans, span_d, 2, span_h, 2, span_w, 2)
    )
    return spread.reshape(chans, 2 * span_d, 2 * span_h, 2 * span_w)


def silu_grad(value):
    sigma = jax.nn.sigmoid(value)
    return sigma * (1.0 + value * (1.0 - sigma))


def reduced(items):
    sizes = [item.size for item in items]
    flat = jnp.concatenate([item.reshape(-1) for item in items]).astype(jnp.bfloat16)
    across = lax.axis_size("height")
    along = lax.axis_size("depth")
    rows = -(-flat.size // (across * 128 * 16)) * 16
    flat = jnp.pad(flat, (0, across * rows * 128 - flat.size))
    parts = lax.all_to_all(flat.reshape(across, rows, 128), "height", 0, 0)
    share = jnp.sum(parts.astype(jnp.float32), axis=0).astype(jnp.bfloat16)
    fine_rows = -(-rows // (along * 8)) * 8
    share = jnp.pad(share, ((0, along * fine_rows - rows), (0, 0)))
    parts = lax.all_to_all(share.reshape(along, fine_rows, 128), "depth", 0, 0)
    own = jnp.sum(parts.astype(jnp.float32), axis=0).astype(jnp.bfloat16)
    share = lax.all_to_all(jnp.broadcast_to(own, (along, fine_rows, 128)), "depth", 0, 0)
    share = share.reshape(along * fine_rows, 128)[:rows]
    total = lax.all_to_all(jnp.broadcast_to(share, (across, rows, 128)), "height", 0, 0)
    total = total.reshape(-1)
    out = []
    at = 0
    for item, size in zip(items, sizes):
        out.append(total[at : at + size].reshape(item.shape).astype(jnp.float32))
        at += size
    return out


def column(vector):
    return vector[:, None, None, None]


def local(
    features,
    kernel_in,
    kernel_down,
    kernel_coarse,
    kernel_up,
    kernel_out,
    projection,
    biases,
    cotangent,
):
    fine = CH_FINE
    middle = CH_MID
    kernel_in = shaped(kernel_in, fine, fine)
    kernel_down = shaped(kernel_down, middle, fine)
    kernel_coarse = shaped(kernel_coarse, middle, middle)
    kernel_up = shaped(kernel_up, middle, middle)
    kernel_out = shaped(kernel_out, fine, fine)
    bias_in = biases[:fine]
    bias_down = biases[fine : fine + middle]
    bias_coarse = biases[fine + middle : fine + 2 * middle]
    bias_up = biases[fine + 2 * middle : fine + 3 * middle]
    bias_out = biases[fine + 3 * middle :]
    bf = jnp.bfloat16
    f32 = jnp.float32
    total_cells = (
        features.shape[1]
        * features.shape[2]
        * features.shape[3]
        * lax.axis_size("depth")
        * lax.axis_size("height")
    )
    scale = 1.0 / math.sqrt(total_cells)
    padded_input = extend(features)
    pre_first = conv_taps(padded_input, kernel_in) + column(bias_in)
    act_first = jax.nn.silu(pre_first).astype(bf)
    pooled_one = (pool_sum(act_first) * 0.125).astype(bf)
    padded_one = extend(pooled_one)
    pre_second = conv_taps(padded_one, kernel_down) + column(bias_down)
    act_second = jax.nn.silu(pre_second).astype(bf)
    pooled_two = (pool_sum(act_second) * 0.125).astype(bf)
    padded_two = extend(pooled_two)
    pre_third = conv_taps(padded_two, kernel_coarse) + column(bias_coarse)
    act_third = jax.nn.silu(pre_third).astype(bf)
    merged = (act_second.astype(f32) + upsample(act_third).astype(f32)).astype(bf)
    padded_merged = extend(merged)
    pre_fourth = conv_taps(padded_merged, kernel_up) + column(bias_up)
    act_fourth = jax.nn.silu(pre_fourth).astype(bf)
    lifted = jnp.einsum("io,idhw->odhw", projection, act_fourth, preferred_element_type=f32)
    skip_sum = (act_first.astype(f32) + upsample(lifted)).astype(bf)
    padded_skip = extend(skip_sum)
    decoded = (conv_taps(padded_skip, kernel_out) + column(bias_out)).astype(bf)
    grad_skip = conv_taps(extend(cotangent), flipped(kernel_out)).astype(bf)
    grad_lift = pool_sum(grad_skip)
    fourth_f32 = act_fourth.astype(f32)
    grad_act4 = jnp.einsum(
        "io,odhw->idhw", projection.astype(f32), grad_lift, precision=lax.Precision.HIGHEST
    )
    grad_pre4 = (grad_act4 * silu_grad(pre_fourth)).astype(bf)
    grad_merged = conv_taps(extend(grad_pre4), flipped(kernel_up))
    grad_pre3 = (pool_sum(grad_merged) * silu_grad(pre_third)).astype(bf)
    grad_pool2 = conv_taps(extend(grad_pre3), flipped(kernel_coarse))
    grad_pre2 = ((grad_merged + upsample(grad_pool2) * 0.125) * silu_grad(pre_second)).astype(bf)
    grad_pool1 = conv_taps(extend(grad_pre2), flipped(kernel_down))
    grad_pre1 = (
        (grad_skip.astype(f32) + upsample(grad_pool1) * 0.125) * silu_grad(pre_first)
    ).astype(bf)
    grad_features = conv_taps(extend(grad_pre1), flipped(kernel_in)).astype(bf)
    local_in = kernel_taps(padded_input, grad_pre1)
    local_down = kernel_taps(padded_one, grad_pre2)
    local_coarse = kernel_taps(padded_two, grad_pre3)
    local_up = kernel_taps(padded_merged, grad_pre4)
    local_out = kernel_taps(padded_skip, cotangent)
    local_projection = jnp.einsum(
        "idhw,odhw->io", fourth_f32, grad_lift, precision=lax.Precision.HIGHEST
    )
    parts = [
        jnp.sum(item.astype(f32), axis=(1, 2, 3))
        for item in (grad_pre1, grad_pre2, grad_pre3, grad_pre4, cotangent)
    ]
    local_biases = jnp.concatenate(parts)
    summed = reduced(
        (local_in, local_down, local_coarse, local_up, local_out, local_projection, local_biases)
    )
    grad_in, grad_down, grad_coarse, grad_up, grad_out, grad_projection, grad_biases = [
        item * scale for item in summed
    ]
    return (
        decoded,
        grad_features,
        grad_in,
        grad_down,
        grad_coarse,
        grad_up,
        grad_out,
        grad_projection,
        grad_biases,
    )


def solution(mesh):
    placed = (
        P(None, "depth", "height", None),
        P(),
        P(),
        P(),
        P(),
        P(),
        P(),
        P(),
        P(None, "depth", "height", None),
    )
    return jax.shard_map(
        local,
        mesh=mesh,
        in_specs=placed,
        out_specs=(
            P(None, "depth", "height", None),
            P(None, "depth", "height", None),
            P(),
            P(),
            P(),
            P(),
            P(),
            P(),
            P(),
        ),
        check_vma=False,
    )
```

```python
import functools
import math

import jax
import jax.numpy as jnp
from jax import lax
from jax.experimental import pallas as pl
from jax.experimental.pallas import tpu as pltpu
from jax.sharding import PartitionSpec as P

CH_FINE = 32
CH_MID = 64
FINE_W = 128
MID_W = 64
COARSE_W = 32
BF = jnp.bfloat16
F32 = jnp.float32


def mm(a, b):
    return lax.dot_general(a, b, (((1,), (0,)), ((), ())), preferred_element_type=F32)


def mm_nt(a, b):
    return lax.dot_general(a, b, (((1,), (1,)), ((), ())), preferred_element_type=F32)


def iota(shape, dim):
    return lax.broadcasted_iota(jnp.int32, shape, dim)


def shifted(x, rows, cells, width):
    if rows == 0 and cells == 0:
        return x
    lanes = x.shape[1]
    step = rows * width + cells
    y = pltpu.roll(x, (-step) % lanes, 1)
    lane = iota((1, lanes), 1)
    keep = None
    if cells:
        cell = lax.rem(lane, width) + cells
        keep = (cell >= 0) & (cell < width)
    if rows:
        at = lane + rows * width
        inside = (at >= 0) & (at < lanes)
        keep = inside if keep is None else keep & inside
    return jnp.where(keep, y, 0.0)


def widened(plane, width):
    wide = plane.astype(F32)
    return jnp.concatenate(
        [shifted(wide, 0, -1, width).astype(BF), plane, shifted(wide, 0, 1, width).astype(BF)], axis=0
    )


def row_taps(plane, width):
    wide = plane.astype(F32)
    return jnp.concatenate(
        [shifted(wide, 1, 0, width).astype(BF), plane, shifted(wide, -1, 0, width).astype(BF)], axis=0
    )


def fold_cells(taps, width):
    ins = taps.shape[0] // 3
    return (
        shifted(taps[:ins], 0, 1, width)
        + taps[ins : 2 * ins]
        + shifted(taps[2 * ins :], 0, -1, width)
    )


def turned(kern):
    side = kern.shape[1]
    eye = (iota((side, side), 0) == iota((side, side), 1)).astype(F32).astype(BF)
    return mm_nt(eye, kern).astype(BF)


def gate(v):
    return 1.0 / (1.0 + jnp.exp(-v))


def split(v):
    high = v.astype(BF)
    return high, (v - high.astype(F32)).astype(BF)


def pool_matrix(lanes, width):
    r = iota((lanes, lanes // 4), 0)
    q = iota((lanes, lanes // 4), 1)
    goal = (r // (2 * width)) * (width // 2) + lax.rem(r, width) // 2
    return (goal == q).astype(F32).astype(BF)


def spread_matrix(lanes, width):
    r = iota((lanes // 4, lanes), 1)
    q = iota((lanes // 4, lanes), 0)
    goal = (r // (2 * width)) * (width // 2) + lax.rem(r, width) // 2
    return (goal == q).astype(F32).astype(BF)


def window_spread():
    r = iota((6 * MID_W, 6 * FINE_W), 0)
    q = iota((6 * MID_W, 6 * FINE_W), 1)
    row = (q // FINE_W + 1) // 2 + 1
    hit = (r // MID_W == row) & (lax.rem(r, MID_W) == lax.rem(q, FINE_W) // 2)
    return hit.astype(F32).astype(BF)


def window(pad_ref, place, at):
    return pad_ref[place, :, pl.ds(pl.multiple_of(128 * at, 128), 384)]


def fill_padded(pad_ref, place, plane):
    chans, lanes = plane.shape
    pad_ref[place, :, 0:128] = jnp.zeros((chans, 128), plane.dtype)
    pad_ref[place, :, 128 : 128 + lanes] = plane
    pad_ref[place, :, 128 + lanes : 256 + lanes] = jnp.zeros((chans, 128), plane.dtype)


def tap_windows(win):
    wide = win.astype(F32)
    cells = [shifted(wide, 0, c - 1, MID_W) for c in range(3)]
    out = []
    for b in range(3):
        start = 128 + (b - 1) * MID_W
        out.append(jnp.concatenate([v[:, start : start + 128] for v in cells], axis=0).astype(BF))
    return out


def gathered(g_ref, place, low, high):
    return jnp.concatenate([g_ref[h, place, low:high, :] for h in range(g_ref.shape[0])], axis=1)


def fine_kernel(nd, nh, idx, xl, xc, xr, kin, kout, bias, act, ds1, gsk, fx, cot, mid, planes, pre, full, gfull, kt):
    dep, hei = idx[0], idx[1]
    for d in range(10):
        src, i = (xl, d) if d < 3 else (xc, d - 3) if d < 7 else (xr, d - 7)
        planes[d] = jnp.concatenate([src[i, h] for h in range(8)], axis=1)
    kt[...] = turned(kout[...])
    pre[...] = jnp.zeros_like(pre)

    def forward(d, carry):
        y = mm(kin[...], widened(planes[d, 0:32, :], FINE_W))
        for a in range(3):
            part = y[96 * a : 96 * a + 32, 0:768]
            for b in (1, 2):
                part += y[96 * a + 32 * b : 96 * a + 32 * b + 32, 128 * b : 128 * b + 768]
            pre[d - a + 2] += part
        return carry

    lax.fori_loop(0, 10, forward, 0)
    h_at = iota((1, 768), 1) // FINE_W - 1 + 4 * hei
    h_in = (h_at >= 0) & (h_at < 4 * nh)

    def finish(d, carry):
        at = 4 * dep + d - 2
        inside = h_in & (at >= 0) & (at < 4 * nd)
        v = pre[d + 2] + bias[...]
        s = gate(v)
        full[d] = jnp.where(inside, v * s, 0.0).astype(BF)
        pre[d + 2] = jnp.where(inside, s * (1.0 + v * (1.0 - s)), 0.0)
        stack = jnp.concatenate(
            [
                planes[d + 2 - a, 32:64, 128 * (2 - b) : 128 * (2 - b) + 768]
                for a in range(3)
                for b in range(3)
            ],
            axis=0,
        )
        gfull[d] = fold_cells(mm(kt[...], stack), FINE_W).astype(BF)
        return carry

    lax.fori_loop(0, 8, finish, 0)
    act[...] = full[1:7]
    gsk[...] = gfull[1:7]
    ds1[...] = pre[3:9]
    fx[...] = planes[2:8, 0:32, 128:896]
    cot[...] = planes[3:7, 32:64, 256:768]
    r = iota((512, 128), 0)
    goal = (r // 256) * 64 + lax.rem(r, 128) // 2
    pooling = (goal == iota((512, 128), 1)).astype(F32).astype(BF)
    for m in range(4):
        one = mm(full[2 * m, :, 128:640], pooling) + mm(full[2 * m + 1, :, 128:640], pooling)
        mid[m, 0:32, :] = (one * 0.125).astype(BF)
        two = mm(gfull[2 * m, :, 128:640], pooling) + mm(gfull[2 * m + 1, :, 128:640], pooling)
        mid[m, 32:64, :] = two.astype(BF)


def down_kernel(g, kdown, bias, out, ds2):
    lanes = 128 * g.shape[0]
    wide = [widened(gathered(g, m, 0, 32), MID_W) for m in range(4)]
    pooled = None
    pooling = pool_matrix(lanes, MID_W)
    for p in range(2):
        pre = None
        for a in range(3):
            y = mm(kdown[192 * a : 192 * a + 192, :], wide[p + a])
            part = shifted(y[0:64], -1, 0, MID_W) + y[64:128] + shifted(y[128:192], 1, 0, MID_W)
            pre = part if pre is None else pre + part
        pre = pre + bias[...]
        s = gate(pre)
        acted = (pre * s).astype(BF)
        out[:, p * lanes : (p + 1) * lanes] = acted
        ds2[:, p * lanes : (p + 1) * lanes] = (s * (1.0 + pre * (1.0 - s))).astype(BF)
        part = mm(acted, pooling)
        pooled = part if pooled is None else pooled + part
    out[:, 2 * lanes :] = (pooled * 0.125).astype(BF)


def core_kernel(nd, idx, own, lf, rt, p2l, p2r, g, kcoarse, kup, proj, b_coarse, b_up, act4, gp4, merged, snd, gs, kt):
    dep = idx[0]
    lanes = 128 * g.shape[0]
    small = lanes // 4
    pools = [p2l[...], lf[:, 2 * lanes :], own[:, 2 * lanes :], rt[:, 2 * lanes :], p2r[...]]
    wide = [widened(v, COARSE_W) for v in pools]
    spreading = spread_matrix(lanes, MID_W)
    ds3 = None
    lifts = []
    for q in range(3):
        pre = None
        for a in range(3):
            y = mm(kcoarse[192 * a : 192 * a + 192, :], wide[q + a])
            part = shifted(y[0:64], -1, 0, COARSE_W) + y[64:128] + shifted(y[128:192], 1, 0, COARSE_W)
            pre = part if pre is None else pre + part
        pre = pre + b_coarse[...]
        s = gate(pre)
        at = dep + q - 1
        acted = jnp.where((at >= 0) & (at < nd), pre * s, 0.0).astype(BF)
        lifts.append(mm(acted, spreading))
        if q == 1:
            ds3 = s * (1.0 + pre * (1.0 - s))
    wide = []
    for k in range(6):
        src = (lf, own, rt)[k // 2]
        start = (k % 2) * lanes
        plane = (src[:, start : start + lanes].astype(F32) + lifts[k // 2]).astype(BF)
        if 1 <= k < 5:
            merged[k - 1] = plane
        wide.append(widened(plane, MID_W))
    kt[...] = turned(kup[...])
    for p in range(4):
        pre = None
        for a in range(3):
            y = mm(kup[192 * a : 192 * a + 192, :], wide[p + a])
            part = shifted(y[0:64], -1, 0, MID_W) + y[64:128] + shifted(y[128:192], 1, 0, MID_W)
            pre = part if pre is None else pre + part
        pre = pre + b_up[...]
        s = gate(pre)
        act4[p] = (pre * s).astype(BF)
        at = 2 * dep + p - 1
        slope = jnp.where((at >= 0) & (at < 2 * nd), s * (1.0 + pre * (1.0 - s)), 0.0)
        grad = (mm(proj[...], gathered(g, p, 32, 64)) * slope).astype(BF)
        if 1 <= p < 3:
            gp4[p - 1] = grad
        gs[p] = row_taps(grad, MID_W)
    pooling = pool_matrix(lanes, MID_W)
    pooled = None
    for q in range(2):
        stack = jnp.concatenate([gs[q + 2 - a] for a in range(3)], axis=0)
        gm = fold_cells(mm(kt[...], stack), MID_W)
        high, low = split(gm)
        snd[:, q * lanes : (q + 1) * lanes] = high
        part = mm(high, pooling) + mm(low, pooling)
        pooled = part if pooled is None else pooled + part
    snd[:, 2 * lanes :] = (pooled * ds3).astype(BF)


def decode_kernel(
    nd, nh, idx, act4, gp4, merged, snd, own, lf, rt, g, act, cot, kout, proj, b_out,
    dec, d_up, d_coarse, d_out, d_proj, d_bias, pad, skip, gpad, acc,
):
    dep, hei = idx[0], idx[1]
    lanes = 128 * g.shape[0]
    small = lanes // 4
    own_at = pl.ds(pl.multiple_of(128 * hei, 128), 128)
    spreading = window_spread()
    h_at = iota((1, 768), 1) // FINE_W - 1 + 4 * hei
    h_in = (h_at >= 0) & (h_at < 4 * nh)
    for p in range(4):
        fill_padded(pad, p, act4[p])
        raised = mm(window(pad, p, hei), spreading).astype(BF)
        lifted = lax.dot_general(proj[...], raised, (((0,), (0,)), ((), ())), preferred_element_type=F32)
        for e in (2 * p - 1, 2 * p):
            if 0 <= e < 6:
                at = 4 * dep + e - 1
                inside = h_in & (at >= 0) & (at < 4 * nd)
                skip[e] = jnp.where(inside, act[e].astype(F32) + lifted, 0.0).astype(BF)
    for k in range(8):
        if 2 <= k < 6:
            plane = cot[k - 2]
            blank = jnp.zeros((32, 128), BF)
            for b in range(3):
                gpad[k, 32 * b : 32 * b + 32, :] = jnp.concatenate(
                    [blank] * b + [plane] + [blank] * (2 - b), axis=1
                )
        else:
            gpad[k] = jnp.zeros((96, 768), BF)
    acc[...] = jnp.zeros_like(acc)
    d_out[...] = jnp.zeros_like(d_out)

    def plane_step(e, carry):
        wide = widened(skip[e], FINE_W)
        y = mm(kout[...], wide)
        for a in range(3):
            part = y[96 * a : 96 * a + 32, 0:512]
            for b in (1, 2):
                part += y[96 * a + 32 * b : 96 * a + 32 * b + 32, 128 * b : 128 * b + 512]
            acc[e - a + 2] += part
        stack = jnp.concatenate([gpad[e + 2], gpad[e + 1], gpad[e]], axis=0)
        d_out[...] += mm_nt(stack, wide)
        return carry

    lax.fori_loop(0, 6, plane_step, 0)
    for d in range(4):
        dec[d] = (acc[d + 2] + b_out[...]).astype(BF)
    grads = jnp.concatenate([gp4[0, :, own_at], gp4[1, :, own_at]], axis=1)
    taps = []
    for p in range(4):
        fill_padded(pad, p, merged[p])
        taps.append(tap_windows(window(pad, p, hei)))
    for a in range(3):
        for b in range(3):
            d_up[3 * a + b] = mm_nt(grads, jnp.concatenate([taps[a][b], taps[a + 1][b]], axis=1))
    acts = jnp.concatenate([act4[1, :, own_at], act4[2, :, own_at]], axis=1)
    lifts = jnp.concatenate([g[hei, 1, 32:64, :], g[hei, 2, 32:64, :]], axis=1)
    d_proj[...] = mm_nt(acts, lifts)
    mine = iota((1, small), 1) // COARSE_W == hei
    third = jnp.where(mine, snd[:, 2 * lanes :].astype(F32), 0.0)
    third_b = third.astype(BF)
    for a, src in enumerate((lf, own, rt)):
        plane = src[:, 2 * lanes :].astype(F32)
        for b in range(3):
            cols = jnp.concatenate(
                [shifted(plane, b - 1, c - 1, COARSE_W).astype(BF) for c in range(3)], axis=0
            )
            d_coarse[3 * a + b] = mm_nt(third_b, cols)
    d_bias[0:64, :] = jnp.broadcast_to(jnp.sum(third, axis=1, keepdims=True), (64, 128))
    d_bias[64:128, :] = jnp.broadcast_to(jnp.sum(grads.astype(F32), axis=1, keepdims=True), (64, 128))
    total = sum(jnp.sum(cot[d].astype(F32), axis=1, keepdims=True) for d in range(4))
    d_bias[128:160, :] = jnp.broadcast_to(total, (32, 128))


def back_kernel(
    idx, own, lf, rt, g3l, g3r, ds_own, ds_lf, ds_rt, g, gsk, ds1, fx, kcoarse, kdown,
    gp1, d_in, d_down, d_bias, pad, pad1, gs2, gpad, kct, kdt,
):
    hei = idx[1]
    lanes = 128 * g.shape[0]
    thirds = [g3l[...], lf[:, 2 * lanes :], own[:, 2 * lanes :], rt[:, 2 * lanes :], g3r[...]]
    taps = [row_taps(v, COARSE_W) for v in thirds]
    kct[...] = turned(kcoarse[...])
    kdt[...] = turned(kdown[...])
    spreading = spread_matrix(lanes, MID_W)
    grads = []
    for q in range(3):
        stack = jnp.concatenate([taps[q + 2 - a] for a in range(3)], axis=0)
        high, low = split(fold_cells(mm(kct[...], stack), COARSE_W))
        lifted = (mm(high, spreading) + mm(low, spreading)) * 0.125
        src, slope = ((lf, ds_lf), (own, ds_own), (rt, ds_rt))[q]
        for k in range(2):
            at = slice(k * lanes, (k + 1) * lanes)
            plane = ((src[:, at].astype(F32) + lifted) * slope[:, at].astype(F32)).astype(BF)
            fill_padded(pad, 0, plane)
            win = window(pad, 0, hei)
            gs2[2 * q + k] = row_taps(win, MID_W)
            if q == 1:
                grads.append(win[:, 128:256])
    raising = window_spread()
    for p in range(4):
        stack = jnp.concatenate([gs2[p + 2 - a] for a in range(3)], axis=0)
        high, low = split(fold_cells(mm(kdt[...], stack), MID_W))
        raised = (mm(high, raising) + mm(low, raising)) * 0.125
        for e in (2 * p - 1, 2 * p):
            if 0 <= e < 6:
                gp1[e] = ((gsk[e].astype(F32) + raised) * ds1[e]).astype(BF)
    taps = []
    for p in range(4):
        fill_padded(pad1, 0, gathered(g, p, 0, 32))
        taps.append(tap_windows(window(pad1, 0, hei)))
    both = jnp.concatenate(grads, axis=1)
    for a in range(3):
        for b in range(3):
            d_down[3 * a + b] = mm_nt(both, jnp.concatenate([taps[a][b], taps[a + 1][b]], axis=1))
    d_bias[32:96, :] = jnp.broadcast_to(jnp.sum(both.astype(F32), axis=1, keepdims=True), (64, 128))
    total = jnp.zeros((32, 1), F32)
    for k in range(8):
        if 2 <= k < 6:
            plane = gp1[k - 1, :, 128:640]
            total += jnp.sum(plane.astype(F32), axis=1, keepdims=True)
            blank = jnp.zeros((32, 128), BF)
            for b in range(3):
                gpad[k, 32 * b : 32 * b + 32, :] = jnp.concatenate(
                    [blank] * b + [plane] + [blank] * (2 - b), axis=1
                )
        else:
            gpad[k] = jnp.zeros((96, 768), BF)
    d_bias[0:32, :] = jnp.broadcast_to(total, (32, 128))
    d_in[...] = jnp.zeros_like(d_in)

    def plane_step(e, carry):
        stack = jnp.concatenate([gpad[e + 2], gpad[e + 1], gpad[e]], axis=0)
        d_in[...] += mm_nt(stack, widened(fx[e], FINE_W))
        return carry

    lax.fori_loop(0, 6, plane_step, 0)


def last_kernel(gp1, kin, out, kt):
    kt[...] = turned(kin[...])
    for d in range(4):
        stack = jnp.concatenate(
            [
                gp1[d + 2 - a, :, 128 * (2 - b) : 128 * (2 - b) + 512]
                for a in range(3)
                for b in range(3)
            ],
            axis=0,
        )
        out[d] = fold_cells(mm(kt[...], stack), FINE_W).astype(BF)


def run(body, outs, scratch, args, smem=0, flops=0, name=None):
    specs = [pl.BlockSpec(memory_space=pltpu.SMEM)] * smem
    specs += [pl.BlockSpec(memory_space=pltpu.VMEM)] * (len(args) - smem)
    moved = sum(a.size * a.dtype.itemsize for a in args) + sum(
        math.prod(s) * jnp.dtype(t).itemsize for s, t in outs
    )
    return pl.pallas_call(
        body,
        out_shape=[jax.ShapeDtypeStruct(s, t) for s, t in outs],
        in_specs=specs,
        out_specs=[pl.BlockSpec(memory_space=pltpu.VMEM)] * len(outs),
        scratch_shapes=[pltpu.VMEM(s, t) for s, t in scratch],
        compiler_params=pltpu.CompilerParams(vmem_limit_bytes=48 * 1024 * 1024),
        cost_estimate=pl.CostEstimate(flops=flops, bytes_accessed=moved, transcendentals=0),
        name=name,
    )(*args)


def reduced(items):
    sizes = [item.size for item in items]
    flat = jnp.concatenate([item.reshape(-1) for item in items]).astype(BF)
    across = lax.axis_size("height")
    along = lax.axis_size("depth")
    rows = -(-flat.size // (across * 128 * 16)) * 16
    flat = jnp.pad(flat, (0, across * rows * 128 - flat.size))
    parts = lax.all_to_all(flat.reshape(across, rows, 128), "height", 0, 0)
    share = jnp.sum(parts.astype(F32), axis=0).astype(BF)
    fine_rows = -(-rows // (along * 8)) * 8
    share = jnp.pad(share, ((0, along * fine_rows - rows), (0, 0)))
    parts = lax.all_to_all(share.reshape(along, fine_rows, 128), "depth", 0, 0)
    own = jnp.sum(parts.astype(F32), axis=0).astype(BF)
    share = lax.all_to_all(jnp.broadcast_to(own, (along, fine_rows, 128)), "depth", 0, 0)
    share = share.reshape(along * fine_rows, 128)[:rows]
    total = lax.all_to_all(jnp.broadcast_to(share, (across, rows, 128)), "height", 0, 0)
    total = total.reshape(-1)
    out = []
    at = 0
    for item, size in zip(items, sizes):
        out.append(total[at : at + size].reshape(item.shape).astype(F32))
        at += size
    return out


def both_ways(axis, to_next, to_last, step=1):
    count = lax.axis_size(axis)
    up = [(i, i + step) for i in range(count - step)]
    down = [(i + step, i) for i in range(count - step)]
    return lax.ppermute(to_next, axis, up), lax.ppermute(to_last, axis, down)


def local(
    features,
    kernel_in,
    kernel_down,
    kernel_coarse,
    kernel_up,
    kernel_out,
    projection,
    biases,
    cotangent,
):
    nd = lax.axis_size("depth")
    nh = lax.axis_size("height")
    lanes = 128 * nh
    small = lanes // 4
    kin = kernel_in.reshape(288, 96)
    kout = kernel_out.reshape(288, 96)
    kdown = kernel_down.reshape(576, 96)
    kcoarse = kernel_coarse.reshape(576, 192)
    kup = kernel_up.reshape(576, 192)
    column = biases[:, None]
    scale = 1.0 / math.sqrt(features.shape[1] * features.shape[2] * features.shape[3] * nd * nh)
    idx = jnp.stack([lax.axis_index("depth"), lax.axis_index("height")]).astype(jnp.int32)

    x = jnp.concatenate([features, cotangent], axis=0).transpose(1, 2, 0, 3)
    low, high = both_ways("height", x[:, 2:4], x[:, 0:2])
    x = jnp.concatenate([low, x, high], axis=1)
    low, high = both_ways("depth", x[1:4], x[0:3])
    act, ds1, gsk, fx, cot, mid = run(
        functools.partial(fine_kernel, nd, nh),
        [
            ((6, 32, 768), BF),
            ((6, 32, 768), F32),
            ((6, 32, 768), BF),
            ((6, 32, 768), BF),
            ((4, 32, 512), BF),
            ((4, 64, 128), BF),
        ],
        [
            ((10, 64, 1024), BF),
            ((12, 32, 768), F32),
            ((8, 32, 768), BF),
            ((8, 32, 768), BF),
            ((96, 288), BF),
        ],
        (idx, low, x, high, kin, kout, column[0:32]),
        smem=1,
        flops=10**9,
        name="fine",
    )
    g = lax.all_to_all(jnp.broadcast_to(mid[None], (nh, 4, 64, 128)), "height", 0, 0)
    own, ds2 = run(
        down_kernel,
        [((64, 2 * lanes + small), BF), ((64, 2 * lanes), BF)],
        [],
        (g, kdown, column[32:96]),
        flops=5 * 10**8,
        name="down",
    )
    lf, rt = both_ways("depth", own, own)
    p2l, p2r = both_ways("depth", own[:, 2 * lanes :], own[:, 2 * lanes :], 2)
    act4, gp4, merged, snd = run(
        functools.partial(core_kernel, nd),
        [
            ((4, 64, lanes), BF),
            ((2, 64, lanes), BF),
            ((4, 64, lanes), BF),
            ((64, 2 * lanes + small), BF),
        ],
        [((4, 192, lanes), BF), ((192, 576), BF)],
        (idx, own, lf, rt, p2l, p2r, g, kcoarse, kup, projection, column[96:160], column[160:224]),
        smem=1,
        flops=3 * 10**9,
        name="core",
    )
    slf, srt = both_ways("depth", snd, snd)
    s2l, s2r = both_ways("depth", snd[:, 2 * lanes :], snd[:, 2 * lanes :], 2)
    dlf, drt = both_ways("depth", ds2, ds2)
    dec, d_up, d_coarse, d_out, d_proj, bias_a = run(
        functools.partial(decode_kernel, nd, nh),
        [
            ((4, 32, 512), BF),
            ((9, 64, 192), F32),
            ((9, 64, 192), F32),
            ((288, 96), F32),
            ((64, 32), F32),
            ((160, 128), F32),
        ],
        [
            ((4, 64, lanes + 256), BF),
            ((6, 32, 768), BF),
            ((8, 96, 768), BF),
            ((8, 32, 512), F32),
        ],
        (idx, act4, gp4, merged, snd, own, lf, rt, g, act, cot, kout, projection, column[224:256]),
        smem=1,
        flops=10**9,
        name="decode",
    )
    gp1, d_in, d_down, bias_b = run(
        back_kernel,
        [((6, 32, 768), BF), ((288, 96), F32), ((9, 64, 96), F32), ((96, 128), F32)],
        [
            ((1, 64, lanes + 256), BF),
            ((1, 32, lanes + 256), BF),
            ((6, 192, 384), BF),
            ((8, 96, 768), BF),
            ((192, 576), BF),
            ((96, 576), BF),
        ],
        (idx, snd, slf, srt, s2l, s2r, ds2, dlf, drt, g, gsk, ds1, fx, kcoarse, kdown),
        smem=1,
        flops=10**9,
        name="back",
    )
    (gfeat,) = run(
        last_kernel,
        [((4, 32, 512), BF)],
        [((96, 288), BF)],
        (gp1, kin),
        flops=10**8,
        name="last",
    )
    sums = jnp.concatenate([bias_b[:, 0], bias_a[:, 0]])
    summed = reduced((d_in, d_down, d_coarse, d_up, d_out, d_proj, sums))
    grads = [item * scale for item in summed]

    def placed(v):
        return v.reshape(4, 32, 4, 128).transpose(1, 0, 2, 3)

    return (
        placed(dec),
        placed(gfeat),
        *[item.reshape(-1) for item in grads[:5]],
        grads[5],
        grads[6],
    )


def solution(mesh):
    placed = (
        P(None, "depth", "height", None),
        P(),
        P(),
        P(),
        P(),
        P(),
        P(),
        P(),
        P(None, "depth", "height", None),
    )
    return jax.shard_map(
        local,
        mesh=mesh,
        in_specs=placed,
        out_specs=(
            P(None, "depth", "height", None),
            P(None, "depth", "height", None),
            P(),
            P(),
            P(),
            P(),
            P(),
            P(),
            P(),
        ),
        check_vma=False,
    )
```
